512 devices in a mesh: replica: 32 (over x, z_lo, core), seq: 16 (over y, z_hi).
Axes of the slice: x: 4, y: 4, z: 16 (z_hi: 4, z_lo: 4; z = z_hi * 4 + z_lo), core: 2. Of those that a mesh axis runs over, the one named last changes fastest.
Arguments:
- query_rows: bfloat16 [32, 2048, 2048], P('replica', 'seq'), may hold values from -110 to 110, as said below
- key_rows: bfloat16 [32, 2048, 2048], P('replica', 'seq'), may hold values from -4 to 4
- value_rows: bfloat16 [32, 2048, 2048], P('replica', 'seq'), may hold values from -6 to 6
- out_grad: bfloat16 [32, 2048, 2048], P('replica', 'seq'), may hold values from -6 to 6
- drift: bfloat16 [32, 3072, 1536], P('replica', 'seq'), may hold values from -12 to 12
- kept_index: int32 [32, 48, 24, 32], P(None, 'seq'), may hold values from 0 to 4095, as said below
Outputs:
- query_grad: bfloat16 [32, 2048, 2048], P('replica', 'seq')
- key_grad: bfloat16 [32, 2048, 2048], P('replica', 'seq')
- value_grad: bfloat16 [32, 2048, 2048], P('replica', 'seq')
- outer_grad: bfloat16 [3072, 1536], P('seq')
The draws below stay inside these ranges and needn't reach their ends.
Inputs may be any that keep to these rules, and one draw needn't show every extreme that they name: `query_rows`: queries follow a normal law clipped at 4 in the shown draw. `kept_index`: for each replica and block the j-th kept position (j from 0 to 31) lies in j * 64 * 2 to (j + 1) * 64 * 2 - 1; positions of one block are thus distinct and rising.
All inputs are finite; a program needn't handle non-finite values.
Results may differ from the reference program's by a relative error of at most 0.011.
Values may be sent and summed in bfloat16 or wider, within the bound.
A program may use at most 64 MiB of HBM per device.

```python
import math
import jax
import jax.numpy as jnp
from jax import lax

D = 3072
COLS = 1536
HEAD = 128
GROUP = 64
KEEP = 32
SEQS = 2
HEADS = 16
SEQ = 2048
LENGTH = 1024
REPLICAS = 32


def shared_rows(key):
    width = HEADS * HEAD
    base_q = jnp.clip(jax.random.normal(jax.random.fold_in(key, 501), (REPLICAS, SEQ, width), jnp.float32), -4.0, 4.0)
    base_k = jnp.clip(jax.random.normal(jax.random.fold_in(key, 502), (REPLICAS, SEQ, width), jnp.float32), -4.0, 4.0)
    return (base_q, base_k)


def draw_query_rows(key, part):
    base_q, base_k = shared_rows(key)
    return base_q.astype(jnp.bfloat16)


def draw_key_rows(key, part):
    base_q, base_k = shared_rows(key)
    return base_k.astype(jnp.bfloat16)


def draw_kept_index(key, part):
    key = jax.random.fold_in(key, 13)
    band = GROUP * GROUP // KEEP
    offsets = jax.random.randint(key, (REPLICAS, D // GROUP, COLS // GROUP, KEEP), 0, band)
    return (offsets + band * jnp.arange(KEEP, dtype=jnp.int32)).astype(jnp.int32)


def steps_of(rng, extent, cuts, smallest, top_value):
    level = 1.0
    for axis_at, shards_of in cuts:
        heights = jax.random.uniform(jax.random.fold_in(jax.random.fold_in(rng, 6), axis_at), (shards_of,), jnp.float32, smallest / len(cuts), top_value / len(cuts))
        level = level * jnp.repeat(jnp.exp(heights), extent[axis_at] // shards_of).reshape((-1,) + (1,) * (len(extent) - 1 - axis_at))
    return level


def normal_values(key, shape, deviation, most, shards=(), kind=jnp.bfloat16):
    loudness = steps_of(key, shape, shards, -0.22, 0.18) if shards else 1.0
    entries = jax.random.normal(key, shape, jnp.float32) * deviation * loudness
    return jnp.minimum(jnp.maximum(entries, -most), most).astype(kind)


def setup_inputs(seed: int = 0) -> dict:
    key_of = jax.random.split(jax.random.key(seed), 7)
    query_rows = draw_query_rows(jax.random.fold_in(key_of[6], 71), 0)
    key_rows = draw_key_rows(jax.random.fold_in(key_of[6], 71), 0)
    value_rows = normal_values(key_of[2], (REPLICAS, SEQ, HEADS * HEAD), 1.0, 6.0, ((0, 32), (1, 16)))
    out_grad = normal_values(key_of[3], (REPLICAS, SEQ, HEADS * HEAD), 1.0, 6.0, ((0, 32), (1, 16)))
    drift = normal_values(key_of[4], (REPLICAS, D, COLS), 2.0, 12.0, ((0, 32), (1, 16)))
    kept_index = draw_kept_index(jax.random.fold_in(key_of[6], 71), 0)
    return dict(query_rows=query_rows, key_rows=key_rows, value_rows=value_rows, out_grad=out_grad, drift=drift, kept_index=kept_index)


def dct_table(size):
    rows = jnp.arange(size)[:, None].astype(jnp.float32)
    cols = jnp.arange(size)[None, :].astype(jnp.float32)
    factor = jnp.where(rows == 0, jnp.sqrt(1.0 / size), jnp.sqrt(2.0 / size))
    return factor * jnp.cos(math.pi * (2.0 * cols + 1.0) * rows / (2.0 * size))

def forward_groups(field, table):
    nrow = field.shape[0] // GROUP
    ncol = field.shape[1] // GROUP
    rowed = jnp.einsum('ij,ajc->aic', table, field.reshape(nrow, GROUP, field.shape[1]), precision=lax.Precision.HIGHEST)
    both = jnp.einsum('ajbk,lk->abjl', rowed.reshape(nrow, GROUP, ncol, GROUP), table, precision=lax.Precision.HIGHEST)
    return both.reshape(nrow, ncol, GROUP * GROUP)

def inverse_groups(coeffs, table):
    nrow, ncol = (coeffs.shape[0], coeffs.shape[1])
    blocks = coeffs.reshape(nrow, ncol, GROUP, GROUP)
    first = jnp.einsum('abil,lk->aibk', blocks, table, precision=lax.Precision.HIGHEST)
    second = jnp.einsum('ij,aibk->ajbk', table, first, precision=lax.Precision.HIGHEST)
    return second.reshape(nrow * GROUP, ncol * GROUP)

def spread(values, index):
    nrow, ncol = (index.shape[-3], index.shape[-2])
    row_ix = jnp.arange(nrow, dtype=jnp.int32)[:, None, None]
    col_ix = jnp.arange(ncol, dtype=jnp.int32)[None, :, None]
    dense = jnp.zeros((nrow, ncol, GROUP * GROUP), jnp.float32)
    return dense.at[row_ix, col_ix, index].add(values)

def head_backward(query, keys_all, values_all, grads):
    length, hcount = (query.shape[0], query.shape[1])
    scale = 1.0 / math.sqrt(HEAD)
    block = min(512, length)
    nblock = length // block
    kf = keys_all.astype(jnp.float32)
    vf = values_all.astype(jnp.float32)

    def step(carry, pieces):
        key_acc, value_acc = carry
        qpart, gpart = pieces
        qf = qpart.astype(jnp.float32)
        gf = gpart.astype(jnp.float32)
        scores = jnp.einsum('qhd,khd->hqk', qf, kf) * scale
        top = lax.optimization_barrier(jnp.max(scores, axis=-1, keepdims=True))
        expo = jnp.exp(scores - top)
        probs = expo / lax.optimization_barrier(jnp.sum(expo, axis=-1, keepdims=True))
        probs_low = probs.astype(jnp.bfloat16)
        plf = probs_low.astype(jnp.float32)
        attended = jnp.einsum('hqk,khd->qhd', plf, vf)
        delta = jnp.transpose(lax.optimization_barrier(jnp.sum(gf * attended, axis=-1)))[:, :, None]
        pgrad = jnp.einsum('qhd,khd->hqk', gf, vf)
        score_grad = (probs * (pgrad - delta)).astype(jnp.bfloat16).astype(jnp.float32)
        qgrad = jnp.einsum('hqk,khd->qhd', score_grad, kf) * scale
        key_acc = key_acc + jnp.einsum('hqk,qhd->khd', score_grad, qf) * scale
        value_acc = value_acc + jnp.einsum('hqk,qhd->khd', plf, gf)
        return ((key_acc, value_acc), qgrad.astype(jnp.bfloat16))
    start = jnp.zeros((length, hcount, HEAD), jnp.float32)
    (key_acc, value_acc), qgrads = lax.scan(step, (start, start), (query.reshape(nblock, block, hcount, HEAD), grads.reshape(nblock, block, hcount, HEAD)))
    return (qgrads.reshape(length, hcount, HEAD), key_acc.astype(jnp.bfloat16), value_acc.astype(jnp.bfloat16))

def window_backward(pieces):
    return head_backward(pieces[0], pieces[1], pieces[2], pieces[3])

def reference(query_rows, key_rows, value_rows, out_grad, drift, kept_index):
    width = query_rows.shape[2]

    def one_replica(pieces):
        shaped = tuple((a.reshape(SEQS, LENGTH, width // HEAD, HEAD) for a in pieces))
        qg, kg, vg = lax.map(window_backward, shaped)
        return (qg.reshape(SEQ, width), kg.reshape(SEQ, width), vg.reshape(SEQ, width))
    query_grad, key_grad, value_grad = lax.map(one_replica, (query_rows, key_rows, value_rows, out_grad))
    table = dct_table(GROUP)

    def kept_of(pieces):
        field, index = pieces
        coeffs = forward_groups(field.astype(jnp.float32), table)
        return jnp.take_along_axis(coeffs, index, axis=-1)
    kept = lax.map(kept_of, (drift, kept_index))
    total = spread(kept, kept_index)
    outer_grad = inverse_groups(total, table).astype(jnp.bfloat16)
    return (query_grad, key_grad, value_grad, outer_grad)
```

```python
import functools
import math

import jax
import jax.numpy as jnp
import numpy as np
from jax import lax
from jax.experimental import pallas as pl
from jax.experimental.pallas import tpu as pltpu
from jax.sharding import PartitionSpec as P

MESH = pl.DeviceIdType.MESH
HEAD = 128
GROUP = 64
NWIN = 8
TOK = 128
LEN = NWIN * TOK
QB = 256
ROWS = 192
COLS = 1536
LANES = 384
F32 = jnp.float32
BF16 = jnp.bfloat16
HIGH = lax.Precision.HIGHEST


def tables():
    i = np.arange(GROUP)[:, None].astype(np.float64)
    j = np.arange(GROUP)[None, :].astype(np.float64)
    c = np.where(i == 0, math.sqrt(1.0 / GROUP), math.sqrt(2.0 / GROUP)) * np.cos(
        math.pi * (2.0 * j + 1.0) * i / (2.0 * GROUP)
    )
    perm = np.concatenate([c[0::2], c[1::2]], axis=0)
    crow = np.kron(np.eye(3), perm)
    ccol = np.kron(np.eye(2), c)
    return crow.astype(np.float32), crow.T.astype(np.float32).copy(), ccol.astype(np.float32)


def kernel(
    q_ref, k_ref, v_ref, g_ref, drift_ref, idx_ref, crow_ref, crowt_ref, ccol_ref,
    dq_ref, dk_ref, dv_ref, outer_ref,
    inb, outb, kt_buf, dk_acc, dv_acc, drift_buf, idx_buf, crow, crowt, ccol, kept, vbuf, outer_buf,
    ss_in, rs_in, ss_out, rs_out, ss_kept, rs_kept, lsem,
):
    rep = lax.axis_index("replica")
    seq = lax.axis_index("seq")
    base = (seq // NWIN) * NWIN
    mine = seq % NWIN
    x = rep // 8
    zlo = (rep // 2) % 4
    core = rep % 2
    m = x * 2 + core
    ins = (q_ref, k_ref, v_ref, g_ref)
    outs = (dq_ref, dk_ref, dv_ref)

    def rep_z(k):
        return x * 8 + ((zlo + k) % 4) * 2 + core

    def rep_m(k):
        m2 = (m + k) % 8
        return (m2 // 2) * 8 + zlo * 2 + m2 % 2

    barrier = pltpu.get_barrier_semaphore()
    for k in range(1, NWIN):
        pl.semaphore_signal(barrier, inc=1, device_id={"seq": base + (mine + k) % NWIN}, device_id_type=MESH)
    for k in range(1, 4):
        pl.semaphore_signal(barrier, inc=1, device_id={"replica": rep_z(k)}, device_id_type=MESH)
    for k in range(1, 8):
        pl.semaphore_signal(barrier, inc=1, device_id={"replica": rep_m(k)}, device_id_type=MESH)

    locals_ = [
        pltpu.make_async_copy(drift_ref.at[0], drift_buf, lsem.at[0]),
        pltpu.make_async_copy(idx_ref.at[rep], idx_buf, lsem.at[1]),
        pltpu.make_async_copy(crow_ref, crow, lsem.at[2]),
        pltpu.make_async_copy(crowt_ref, crowt, lsem.at[3]),
        pltpu.make_async_copy(ccol_ref, ccol, lsem.at[4]),
    ]
    for c in locals_:
        c.start()
    my_rows = pl.ds(pl.multiple_of(mine * TOK, TOK), TOK)
    own = []
    for h in range(2):
        for a in range(4):
            c = pltpu.make_async_copy(
                ins[a].at[0, :, pl.ds(pl.multiple_of(mine * 256 + h * HEAD, HEAD), HEAD)],
                inb.at[h, a, my_rows, :],
                rs_in.at[h, a],
            )
            c.start()

    pl.semaphore_wait(barrier, 7 + 3 + 7)

    for h in range(2):
        for a in range(4):

            def send(s, carry, h=h, a=a):
                to = (mine + s) % NWIN
                pltpu.make_async_remote_copy(
                    src_ref=ins[a].at[0, :, pl.ds(pl.multiple_of(to * 256 + h * HEAD, HEAD), HEAD)],
                    dst_ref=inb.at[h, a, my_rows, :],
                    send_sem=ss_in.at[a],
                    recv_sem=rs_in.at[h, a],
                    device_id={"seq": base + to},
                    device_id_type=MESH,
                ).start()
                return carry

            lax.fori_loop(1, NWIN, send, 0)

    for c in locals_:
        c.wait()
    lane = lax.broadcasted_iota(jnp.int32, (1, LANES), 1)
    tile32 = jnp.where(
        lax.broadcasted_iota(jnp.int32, (32, LANES), 0) == lax.broadcasted_iota(jnp.int32, (32, LANES), 1) % 32,
        1.0,
        0.0,
    ).astype(BF16)
    off = jnp.zeros((12, LANES), F32)
    slot_base = lax.broadcasted_iota(jnp.int32, (12, 32), 1) * 128
    for bm in range(2):
        for a in range(3):
            o = (idx_buf[a, bm * 12 : bm * 12 + 12, :] - slot_base).astype(F32).astype(BF16)
            tiled = jnp.dot(o, tile32, preferred_element_type=F32)
            off = jnp.where(lane // 64 == bm * 3 + a, tiled, off)
    off = off - ((lane // 32) % 2 * GROUP).astype(F32)
    kept[m, zlo, 0] = jnp.zeros((16, LANES), F32)
    kept[m, zlo, 1] = jnp.zeros((16, LANES), F32)
    kept[m, zlo, 1, 0:12, :] = off
    sub = lax.broadcasted_iota(jnp.int32, (GROUP, LANES), 0).astype(F32)

    def forward(t, carry):
        at = pl.multiple_of(t * 128, 128)
        pieces = []
        for bm in range(2):
            xt = drift_buf[:, pl.ds(at + bm * 768, 128)].astype(F32)
            pieces.append(jnp.dot(crow[...], xt, precision=HIGH, preferred_element_type=F32))
        y = jnp.concatenate(pieces, axis=0)
        u = lax.dot_general(ccol[...], y, (((1,), (1,)), ((), ())), precision=HIGH, preferred_element_type=F32)
        for bl in range(2):
            row = kept[m, zlo, 1, pl.ds(t * 2 + bl, 1), :]
            hit = jnp.where(sub == row, u[bl * GROUP : (bl + 1) * GROUP, :], 0.0)
            kept[m, zlo, 0, pl.ds(t * 2 + bl, 1), :] = jnp.sum(hit, axis=0, keepdims=True)
        return carry

    lax.fori_loop(0, 6, forward, 0)
    for k in range(1, 4):
        pltpu.make_async_remote_copy(
            src_ref=kept.at[m, zlo],
            dst_ref=kept.at[m, zlo],
            send_sem=ss_kept.at[0],
            recv_sem=rs_kept.at[0],
            device_id={"replica": rep_z(k)},
            device_id_type=MESH,
        ).start()

    scale = 1.0 / math.sqrt(HEAD)
    my_cols = lambda h: pl.ds(pl.multiple_of(mine * 256 + h * HEAD, HEAD), HEAD)

    def give(h, a, i):
        rows = pl.ds(pl.multiple_of(i * TOK, TOK), TOK)

        @pl.when(i == mine)
        def _():
            pltpu.make_async_copy(outb.at[h, a, rows, :], outs[a].at[0, :, my_cols(h)], rs_out.at[a]).start()

        @pl.when(i != mine)
        def _():
            pltpu.make_async_remote_copy(
                src_ref=outb.at[h, a, rows, :],
                dst_ref=outs[a].at[0, :, my_cols(h)],
                send_sem=ss_out.at[a],
                recv_sem=rs_out.at[a],
                device_id={"seq": base + i},
                device_id_type=MESH,
            ).start()

    def attend(h):
        for a in range(4):
            pltpu.make_async_copy(inb.at[h, a], inb.at[h, a], rs_in.at[h, a]).wait()
        kt_buf[...] = jnp.transpose(inb[h, 1].astype(F32)).astype(BF16)
        dk_acc[...] = jnp.zeros_like(dk_acc)
        dv_acc[...] = jnp.zeros_like(dv_acc)

        def step(b, carry):
            rows = pl.ds(pl.multiple_of(b * QB, QB), QB)
            qb = inb[h, 0, rows, :]
            gb = inb[h, 3, rows, :]
            nt = (((1,), (1,)), ((), ()))
            s = lax.dot_general(inb[h, 1], qb, nt, preferred_element_type=F32)
            top = jnp.max(s, axis=0, keepdims=True)
            e = jnp.exp((s - top) * scale)
            p = e * (1.0 / jnp.sum(e, axis=0, keepdims=True))
            low = p.astype(BF16)
            d = lax.dot_general(inb[h, 2], gb, nt, preferred_element_type=F32)
            delta = jnp.sum(low.astype(F32) * d, axis=0, keepdims=True)
            sg = (p * (d - delta)).astype(BF16)
            dqt = jnp.dot(kt_buf[...], sg, preferred_element_type=F32) * scale
            outb[h, 0, rows, :] = jnp.transpose(dqt).astype(BF16)
            dv_acc[...] += jnp.dot(low, gb, preferred_element_type=F32)
            dk_acc[...] += jnp.dot(sg, qb, preferred_element_type=F32)
            for u in range(QB // TOK):
                give(h, 0, b * (QB // TOK) + u)
            return carry

        lax.fori_loop(0, LEN // QB, step, 0)
        outb[h, 1] = (dk_acc[...] * scale).astype(BF16)
        outb[h, 2] = dv_acc[...].astype(BF16)

        def rest(i, carry):
            give(h, 1, i)
            give(h, 2, i)
            return carry

        lax.fori_loop(0, NWIN, rest, 0)

    attend(0)

    pltpu.make_async_copy(kept.at[m, 0:3], kept.at[m, 0:3], rs_kept.at[0]).wait()
    for k in range(1, 8):
        pltpu.make_async_remote_copy(
            src_ref=kept.at[m],
            dst_ref=kept.at[m],
            send_sem=ss_kept.at[1],
            recv_sem=rs_kept.at[1],
            device_id={"replica": rep_m(k)},
            device_id_type=MESH,
        ).start()

    attend(1)

    pltpu.make_async_copy(kept.at[0:7], kept.at[0:7], rs_kept.at[1]).wait()

    def backward(t, carry):
        at = pl.multiple_of(t * 128, 128)
        zs = []
        for bl in range(2):

            def add(r, z):
                one = pl.ds(t * 2 + bl, 1)
                for s in range(4):
                    z = z + jnp.where(sub == kept[r, s, 1, one, :], kept[r, s, 0, one, :], 0.0)
                return z

            zs.append(lax.fori_loop(0, 8, add, jnp.zeros((GROUP, LANES), F32)))
        z = jnp.transpose(jnp.concatenate(zs, axis=0))
        w = jnp.dot(z, ccol[...], precision=HIGH, preferred_element_type=F32)
        for bm in range(2):
            o = jnp.dot(crowt[...], w[bm * ROWS : (bm + 1) * ROWS, :], precision=HIGH, preferred_element_type=F32)
            outer_buf[:, pl.ds(at + bm * 768, 128)] = o.astype(BF16)
        return carry

    lax.fori_loop(0, 6, backward, 0)
    last = pltpu.make_async_copy(outer_buf, outer_ref, lsem.at[5])
    last.start()

    part = pl.ds(0, 14 * HEAD)
    for a in range(4):
        pltpu.make_async_copy(ins[a].at[0, :, part], ins[a].at[0, :, part], ss_in.at[a]).wait()
    pltpu.make_async_copy(kept.at[0, 0:3], kept.at[0, 0:3], ss_kept.at[0]).wait()
    pltpu.make_async_copy(kept.at[0:7], kept.at[0:7], ss_kept.at[1]).wait()
    for a in range(3):
        pltpu.make_async_copy(outs[a].at[0, :, part], outs[a].at[0, :, part], ss_out.at[a]).wait()
    for a in range(3):
        pltpu.make_async_copy(outs[a].at[0], outs[a].at[0], rs_out.at[a]).wait()
    last.wait()


def on_device(query_rows, key_rows, value_rows, out_grad, drift, kept_index):
    crow, crowt, ccol = (jnp.asarray(t) for t in tables())
    anyspec = pl.BlockSpec(memory_space=pl.ANY)
    rows = jax.ShapeDtypeStruct((1, TOK, 2048), BF16)
    return pl.pallas_call(
        kernel,
        out_shape=(rows, rows, rows, jax.ShapeDtypeStruct((ROWS, COLS), BF16)),
        in_specs=[anyspec] * 9,
        out_specs=[anyspec] * 4,
        scratch_shapes=[
            pltpu.VMEM((2, 4, LEN, HEAD), BF16),
            pltpu.VMEM((2, 3, LEN, HEAD), BF16),
            pltpu.VMEM((HEAD, LEN), BF16),
            pltpu.VMEM((LEN, HEAD), F32),
            pltpu.VMEM((LEN, HEAD), F32),
            pltpu.VMEM((ROWS, COLS), BF16),
            pltpu.VMEM((3, 24, 32), jnp.int32),
            pltpu.VMEM((ROWS, ROWS), F32),
            pltpu.VMEM((ROWS, ROWS), F32),
            pltpu.VMEM((128, 128), F32),
            pltpu.VMEM((8, 4, 2, 16, LANES), F32),
            pltpu.VMEM((8, 128), F32),
            pltpu.VMEM((ROWS, COLS), BF16),
            pltpu.SemaphoreType.DMA((4,)),
            pltpu.SemaphoreType.DMA((2, 4)),
            pltpu.SemaphoreType.DMA((3,)),
            pltpu.SemaphoreType.DMA((3,)),
            pltpu.SemaphoreType.DMA((2,)),
            pltpu.SemaphoreType.DMA((2,)),
            pltpu.SemaphoreType.DMA((6,)),
        ],
        compiler_params=pltpu.CompilerParams(
            collective_id=0, has_side_effects=True, vmem_limit_bytes=48 << 20
        ),
    )(query_rows, key_rows, value_rows, out_grad, drift, kept_index, crow, crowt, ccol)


def solution(mesh):
    tokens = P("replica", "seq", None)
    return jax.shard_map(
        on_device,
        mesh=mesh,
        in_specs=(tokens, tokens, tokens, tokens, tokens, P(None, "seq", None, None)),
        out_specs=(tokens, tokens, tokens, P("seq", None)),
        check_vma=False,
    )
```

```python
import functools
import math

import jax
import jax.numpy as jnp
import numpy as np
from jax import lax
from jax.experimental import pallas as pl
from jax.experimental.pallas import tpu as pltpu
from jax.sharding import PartitionSpec as P

MESH = pl.DeviceIdType.MESH
HEAD = 128
GROUP = 64
NWIN = 8
TOK = 128
LEN = NWIN * TOK
WIDE = 2 * HEAD
QB = 256
ROWS = 192
COLS = 1536
LANES = 384
F32 = jnp.float32
BF16 = jnp.bfloat16
HIGH = lax.Precision.HIGHEST


def tables():
    i = np.arange(GROUP)[:, None].astype(np.float64)
    j = np.arange(GROUP)[None, :].astype(np.float64)
    c = np.where(i == 0, math.sqrt(1.0 / GROUP), math.sqrt(2.0 / GROUP)) * np.cos(
        math.pi * (2.0 * j + 1.0) * i / (2.0 * GROUP)
    )
    perm = np.concatenate([c[0::2], c[1::2]], axis=0)
    crow = np.kron(np.eye(3), perm)
    ccol = np.kron(np.eye(2), c)
    return crow.astype(np.float32), crow.T.astype(np.float32).copy(), ccol.astype(np.float32)


def kernel(
    q_ref, k_ref, v_ref, g_ref, drift_ref, idx_ref, crow_ref, crowt_ref, ccol_ref,
    dq_ref, dk_ref, dv_ref, outer_ref,
    inb, outb, kt_buf, dk_acc, dv_acc, drift_buf, idx_buf, crow, crowt, ccol, kept, picked, place, wide, outer_buf,
    ss_in, rs_kv, rs_q, rs_g, ss_out, rs_out, ss_kept, rs_kept, lsem,
):
    rep = lax.axis_index("replica")
    seq = lax.axis_index("seq")
    base = (seq // NWIN) * NWIN
    mine = seq % NWIN
    pair = mine // 2
    x = rep // 8
    zlo = (rep // 2) % 4
    core = rep % 2
    m = x * 2 + core
    ins = (q_ref, k_ref, v_ref, g_ref)
    outs = (dq_ref, dk_ref, dv_ref)

    def rep_z(k):
        return x * 8 + ((zlo + k) % 4) * 2 + core

    def rep_m(k):
        m2 = (m + k) % 8
        return (m2 // 2) * 8 + zlo * 2 + m2 % 2

    def rows_of(i):
        return pl.ds(pl.multiple_of(i * TOK, TOK), TOK)

    def cols_of(i):
        return pl.ds(pl.multiple_of(i * WIDE, WIDE), WIDE)

    barrier = pltpu.get_barrier_semaphore()
    for k in range(1, NWIN):
        pl.semaphore_signal(barrier, inc=1, device_id={"seq": base + (mine + k) % NWIN}, device_id_type=MESH)
    for k in range(1, 4):
        pl.semaphore_signal(barrier, inc=1, device_id={"replica": rep_z(k)}, device_id_type=MESH)
    for k in range(1, 8):
        pl.semaphore_signal(barrier, inc=1, device_id={"replica": rep_m(k)}, device_id_type=MESH)

    locals_ = [
        pltpu.make_async_copy(drift_ref.at[0], drift_buf, lsem.at[0]),
        pltpu.make_async_copy(idx_ref, idx_buf, lsem.at[1]),
        pltpu.make_async_copy(crow_ref, crow, lsem.at[2]),
        pltpu.make_async_copy(crowt_ref, crowt, lsem.at[3]),
        pltpu.make_async_copy(ccol_ref, ccol, lsem.at[4]),
    ]
    for c in locals_:
        c.start()

    def arrival(a):
        return (rs_q.at[mine], rs_kv.at[0], rs_kv.at[1], rs_g.at[mine])[a]

    for a in range(4):
        pltpu.make_async_copy(ins[a].at[0, :, cols_of(mine)], inb.at[a, rows_of(mine), :], arrival(a)).start()

    pl.semaphore_wait(barrier, 7 + 3 + 7)

    def send(a, to):
        pltpu.make_async_remote_copy(
            src_ref=ins[a].at[0, :, cols_of(to)],
            dst_ref=inb.at[a, rows_of(mine), :],
            send_sem=ss_in.at[a],
            recv_sem=arrival(a),
            device_id={"seq": base + to},
            device_id_type=MESH,
        ).start()

    mate = pair * 2 + 1 - mine % 2

    def others(group):
        for a in group:
            send(a, mate)

        def more(n, carry):
            to = ((pair + 4 - n // 2) % 4) * 2 + n % 2
            for a in group:
                send(a, to)
            return carry

        lax.fori_loop(2, NWIN, more, 0)

    others((1, 2))
    others((0, 3))

    for c in locals_:
        c.wait()
    lane = lax.broadcasted_iota(jnp.int32, (1, LANES), 1)
    parity = ((lane // 32) % 2 * GROUP).astype(F32)
    first_half = lane < ROWS
    slot_base = lax.broadcasted_iota(jnp.int32, (32 * 24, 32), 1) * 128
    jrow = lax.broadcasted_iota(jnp.int32, (32, LANES), 0)
    jlane = lax.broadcasted_iota(jnp.int32, (32, LANES), 1)
    spots = jnp.zeros((32 * 24, LANES), F32) - parity
    for a in range(3):
        o = (idx_buf[:, a].reshape(32 * 24, 32) - slot_base).astype(F32).astype(BF16)
        at_a = jnp.where((jrow == jlane % 32) & ((jlane // 64) % 3 == a), 1.0, 0.0).astype(BF16)
        spots = spots + jnp.dot(o, at_a, preferred_element_type=F32)
    place[...] = spots.reshape(32, 24, LANES)
    sub = lax.broadcasted_iota(jnp.int32, (GROUP, LANES), 0).astype(F32)

    def halves(ref, r, row):
        return jnp.where(first_half, ref[r, pl.ds(row, 1), :], ref[r, pl.ds(row + 12, 1), :])

    def forward(t, carry):
        at = pl.multiple_of(t * 128, 128)
        pieces = []
        for bm in range(2):
            xt = drift_buf[:, pl.ds(at + bm * 768, 128)].astype(F32)
            pieces.append(jnp.dot(crow[...], xt, precision=HIGH, preferred_element_type=F32))
        y = jnp.concatenate(pieces, axis=0)
        u = lax.dot_general(ccol[...], y, (((1,), (1,)), ((), ())), precision=HIGH, preferred_element_type=F32)
        for bl in range(2):
            hit = jnp.where(sub == halves(place, rep, t * 2 + bl), u[bl * GROUP : (bl + 1) * GROUP, :], 0.0)
            picked[pl.ds(t * 2 + bl, 1), :] = jnp.sum(hit, axis=0, keepdims=True)
        return carry

    lax.fori_loop(0, 6, forward, 0)
    wl = lax.broadcasted_iota(jnp.int32, (LANES, 128), 0)
    nl = lax.broadcasted_iota(jnp.int32, (LANES, 128), 1)
    same = ((wl // 64) % 3 == nl // 32) & (wl % 32 == nl % 32)
    for bm in range(2):
        gather = jnp.where(same & (wl // ROWS == bm), 1.0, 0.0)
        kept[m, zlo, bm * 12 : bm * 12 + 12, :] = jnp.dot(
            picked[0:12, :], gather, precision=HIGH, preferred_element_type=F32
        )
    for k in range(1, 4):
        pltpu.make_async_remote_copy(
            src_ref=kept.at[m, zlo],
            dst_ref=kept.at[m, zlo],
            send_sem=ss_kept.at[0],
            recv_sem=rs_kept.at[0],
            device_id={"replica": rep_z(k)},
            device_id_type=MESH,
        ).start()

    scale = 1.0 / math.sqrt(HEAD)
    nt = (((1,), (1,)), ((), ()))

    def give(a, i):
        @pl.when(i == mine)
        def _():
            pltpu.make_async_copy(outb.at[a, rows_of(i), :], outs[a].at[0, :, cols_of(mine)], rs_out.at[a]).start()

        @pl.when(i != mine)
        def _():
            pltpu.make_async_remote_copy(
                src_ref=outb.at[a, rows_of(i), :],
                dst_ref=outs[a].at[0, :, cols_of(mine)],
                send_sem=ss_out.at[a],
                recv_sem=rs_out.at[a],
                device_id={"seq": base + i},
                device_id_type=MESH,
            ).start()

    for a in (1, 2):
        pltpu.make_async_copy(inb.at[a], inb.at[a], rs_kv.at[a - 1]).wait()
    for h in range(2):
        of_head = slice(h * HEAD, (h + 1) * HEAD)
        kt_buf[h] = jnp.transpose(inb[1, :, of_head].astype(F32)).astype(BF16)
    dk_acc[...] = jnp.zeros_like(dk_acc)
    dv_acc[...] = jnp.zeros_like(dv_acc)

    pltpu.make_async_copy(kept.at[m, 0:3], kept.at[m, 0:3], rs_kept.at[0]).wait()
    for k in range(1, 8):
        pltpu.make_async_remote_copy(
            src_ref=kept.at[m],
            dst_ref=kept.at[m],
            send_sem=ss_kept.at[1],
            recv_sem=rs_kept.at[1],
            device_id={"replica": rep_m(k)},
            device_id_type=MESH,
        ).start()

    def step(n, carry):
        b = (pair + n) % 4
        for u in range(2):
            i = b * 2 + u
            pltpu.make_async_copy(inb.at[0, rows_of(i)], inb.at[0, rows_of(i)], rs_q.at[i]).wait()
            pltpu.make_async_copy(inb.at[3, rows_of(i)], inb.at[3, rows_of(i)], rs_g.at[i]).wait()
        rows = pl.ds(pl.multiple_of(b * QB, QB), QB)
        for h in range(2):
            of_head = slice(h * HEAD, (h + 1) * HEAD)
            qb = inb[0, rows, of_head]
            gb = inb[3, rows, of_head]
            s = lax.dot_general(inb[1, :, of_head], qb, nt, preferred_element_type=F32)
            top = jnp.max(s, axis=0, keepdims=True)
            e = jnp.exp((s - top) * scale)
            p = e * (1.0 / jnp.sum(e, axis=0, keepdims=True))
            low = p.astype(BF16)
            d = lax.dot_general(inb[2, :, of_head], gb, nt, preferred_element_type=F32)
            delta = jnp.sum(low.astype(F32) * d, axis=0, keepdims=True)
            sg = (p * (d - delta)).astype(BF16)
            dqt = jnp.dot(kt_buf[h], sg, preferred_element_type=F32) * scale
            outb[0, rows, of_head] = jnp.transpose(dqt).astype(BF16)
            dv_acc[h] += jnp.dot(low, gb, preferred_element_type=F32)
            dk_acc[h] += jnp.dot(sg, qb, preferred_element_type=F32)
        for u in range(2):
            give(0, b * 2 + u)
        return carry

    lax.fori_loop(0, LEN // QB, step, 0)
    for h in range(2):
        of_head = slice(h * HEAD, (h + 1) * HEAD)
        outb[1, :, of_head] = (dk_acc[h] * scale).astype(BF16)
        outb[2, :, of_head] = dv_acc[h].astype(BF16)

    def rest(n, carry):
        i = ((pair + n // 2) % 4) * 2 + n % 2
        give(1, i)
        give(2, i)
        return carry

    lax.fori_loop(0, NWIN, rest, 0)

    pltpu.make_async_copy(kept.at[0:7], kept.at[0:7], rs_kept.at[1]).wait()
    nr = lax.broadcasted_iota(jnp.int32, (128, LANES), 0)
    wr = lax.broadcasted_iota(jnp.int32, (128, LANES), 1)
    widen = jnp.where(((wr // 64) % 3 == nr // 32) & (wr % 32 == nr % 32), 1.0, 0.0)

    def spread_out(i, carry):
        some = kept[i].reshape(4 * 24, 128)
        wide[pl.ds(i * 4, 4)] = jnp.dot(some, widen, precision=HIGH, preferred_element_type=F32).reshape(4, 24, LANES)
        return carry

    lax.fori_loop(0, 8, spread_out, 0)

    def backward(t, carry):
        at = pl.multiple_of(t * 128, 128)
        zs = []
        for bl in range(2):

            def add(i, z):
                for r in range(8):
                    slot = i * 8 + (r % 2) * 4 + r // 2
                    hit = sub == halves(place, i * 8 + r, t * 2 + bl)
                    z = z + jnp.where(hit, halves(wide, slot, t * 2 + bl), 0.0)
                return z

            zs.append(lax.fori_loop(0, 4, add, jnp.zeros((GROUP, LANES), F32)))
        z = jnp.transpose(jnp.concatenate(zs, axis=0))
        w = jnp.dot(z, ccol[...], precision=HIGH, preferred_element_type=F32)
        for bm in range(2):
            o = jnp.dot(crowt[...], w[bm * ROWS : (bm + 1) * ROWS, :], precision=HIGH, preferred_element_type=F32)
            outer_buf[:, pl.ds(at + bm * 768, 128)] = o.astype(BF16)
        return carry

    lax.fori_loop(0, 6, backward, 0)
    last = pltpu.make_async_copy(outer_buf, outer_ref, lsem.at[5])
    last.start()

    part = pl.ds(0, 7 * WIDE)
    for a in range(4):
        pltpu.make_async_copy(ins[a].at[0, :, part], ins[a].at[0, :, part], ss_in.at[a]).wait()
    pltpu.make_async_copy(kept.at[0, 0:3], kept.at[0, 0:3], ss_kept.at[0]).wait()
    pltpu.make_async_copy(kept.at[0:7], kept.at[0:7], ss_kept.at[1]).wait()
    for a in range(3):
        pltpu.make_async_copy(outs[a].at[0, :, part], outs[a].at[0, :, part], ss_out.at[a]).wait()
    for a in range(3):
        pltpu.make_async_copy(outs[a].at[0], outs[a].at[0], rs_out.at[a]).wait()
    last.wait()


def on_device(query_rows, key_rows, value_rows, out_grad, drift, kept_index):
    crow, crowt, ccol = (jnp.asarray(t) for t in tables())
    anyspec = pl.BlockSpec(memory_space=pl.ANY)
    rows = jax.ShapeDtypeStruct((1, TOK, 2048), BF16)
    return pl.pallas_call(
        kernel,
        out_shape=(rows, rows, rows, jax.ShapeDtypeStruct((ROWS, COLS), BF16)),
        in_specs=[anyspec] * 9,
        out_specs=[anyspec] * 4,
        scratch_shapes=[
            pltpu.VMEM((4, LEN, WIDE), BF16),
            pltpu.VMEM((3, LEN, WIDE), BF16),
            pltpu.VMEM((2, HEAD, LEN), BF16),
            pltpu.VMEM((2, LEN, HEAD), F32),
            pltpu.VMEM((2, LEN, HEAD), F32),
            pltpu.VMEM((ROWS, COLS), BF16),
            pltpu.VMEM((32, 3, 24, 32), jnp.int32),
            pltpu.VMEM((ROWS, ROWS), F32),
            pltpu.VMEM((ROWS, ROWS), F32),
            pltpu.VMEM((128, 128), F32),
            pltpu.VMEM((8, 4, 24, 128), F32),
            pltpu.VMEM((16, LANES), F32),
            pltpu.VMEM((32, 24, LANES), F32),
            pltpu.VMEM((32, 24, LANES), F32),
            pltpu.VMEM((ROWS, COLS), BF16),
            pltpu.SemaphoreType.DMA((4,)),
            pltpu.SemaphoreType.DMA((2,)),
            pltpu.SemaphoreType.DMA((NWIN,)),
            pltpu.SemaphoreType.DMA((NWIN,)),
            pltpu.SemaphoreType.DMA((3,)),
            pltpu.SemaphoreType.DMA((3,)),
            pltpu.SemaphoreType.DMA((2,)),
            pltpu.SemaphoreType.DMA((2,)),
            pltpu.SemaphoreType.DMA((6,)),
        ],
        compiler_params=pltpu.CompilerParams(
            collective_id=0, has_side_effects=True, vmem_limit_bytes=63 << 20
        ),
    )(query_rows, key_rows, value_rows, out_grad, drift, kept_index, crow, crowt, ccol)


def solution(mesh):
    tokens = P("replica", "seq", None)
    return jax.shard_map(
        on_device,
        mesh=mesh,
        in_specs=(tokens, tokens, tokens, tokens, tokens, P(None, "seq", None, None)),
        out_specs=(tokens, tokens, tokens, P("seq", None)),
        check_vma=False,
    )
```

```python
import functools
import math

import jax
import jax.numpy as jnp
import numpy as np
from jax import lax
from jax.experimental import pallas as pl
from jax.experimental.pallas import tpu as pltpu
from jax.sharding import PartitionSpec as P

MESH = pl.DeviceIdType.MESH
HEAD = 128
GROUP = 64
NWIN = 8
TOK = 128
LEN = NWIN * TOK
WIDE = 2 * HEAD
QB = 256
ROWS = 192
COLS = 1536
LANES = 384
F32 = jnp.float32
BF16 = jnp.bfloat16
HIGH = lax.Precision.HIGHEST


def tables():
    i = np.arange(GROUP)[:, None].astype(np.float64)
    j = np.arange(GROUP)[None, :].astype(np.float64)
    c = np.where(i == 0, math.sqrt(1.0 / GROUP), math.sqrt(2.0 / GROUP)) * np.cos(
        math.pi * (2.0 * j + 1.0) * i / (2.0 * GROUP)
    )
    perm = np.concatenate([c[0::2], c[1::2]], axis=0)
    crow = np.kron(np.eye(3), perm)
    ccol = np.kron(np.eye(2), c)
    return crow.astype(np.float32), crow.T.astype(np.float32).copy(), ccol.astype(np.float32)


def kernel(
    q_ref, k_ref, v_ref, g_ref, drift_ref, idx_ref, crow_ref, crowt_ref, ccol_ref,
    dq_ref, dk_ref, dv_ref, outer_ref,
    inb, outb, kt_buf, dk_acc, dv_acc, drift_buf, idx_buf, crow, crowt, ccol, kept, picked, place, wide, outer_buf,
    ss_in, rs_kv, rs_q, rs_g, ss_out, rs_out, ss_kept, rs_kept, lsem,
):
    rep = lax.axis_index("replica")
    seq = lax.axis_index("seq")
    base = (seq // NWIN) * NWIN
    mine = seq % NWIN
    pair = mine // 2
    x = rep // 8
    zlo = (rep // 2) % 4
    core = rep % 2
    m = x * 2 + core
    ins = (q_ref, k_ref, v_ref, g_ref)
    outs = (dq_ref, dk_ref, dv_ref)

    def rep_z(k):
        return x * 8 + ((zlo + k) % 4) * 2 + core

    def rep_m(k):
        m2 = (m + k) % 8
        return (m2 // 2) * 8 + zlo * 2 + m2 % 2

    def rows_of(i):
        return pl.ds(pl.multiple_of(i * TOK, TOK), TOK)

    def cols_of(i):
        return pl.ds(pl.multiple_of(i * WIDE, WIDE), WIDE)

    barrier = pltpu.get_barrier_semaphore()
    for k in range(1, NWIN):
        pl.semaphore_signal(barrier, inc=1, device_id={"seq": base + (mine + k) % NWIN}, device_id_type=MESH)
    for k in range(1, 4):
        pl.semaphore_signal(barrier, inc=1, device_id={"replica": rep_z(k)}, device_id_type=MESH)
    for k in range(1, 8):
        pl.semaphore_signal(barrier, inc=1, device_id={"replica": rep_m(k)}, device_id_type=MESH)

    locals_ = [
        pltpu.make_async_copy(drift_ref.at[0], drift_buf, lsem.at[0]),
        pltpu.make_async_copy(idx_ref, idx_buf, lsem.at[1]),
        pltpu.make_async_copy(crow_ref, crow, lsem.at[2]),
        pltpu.make_async_copy(crowt_ref, crowt, lsem.at[3]),
        pltpu.make_async_copy(ccol_ref, ccol, lsem.at[4]),
    ]
    for c in locals_:
        c.start()

    def arrival(a):
        return (rs_q.at[mine], rs_kv.at[0], rs_kv.at[1], rs_g.at[mine])[a]

    for a in range(4):
        pltpu.make_async_copy(ins[a].at[0, :, cols_of(mine)], inb.at[a, rows_of(mine), :], arrival(a)).start()

    pl.semaphore_wait(barrier, 7 + 3 + 7)

    def send(a, to):
        pltpu.make_async_remote_copy(
            src_ref=ins[a].at[0, :, cols_of(to)],
            dst_ref=inb.at[a, rows_of(mine), :],
            send_sem=ss_in.at[a],
            recv_sem=arrival(a),
            device_id={"seq": base + to},
            device_id_type=MESH,
        ).start()

    mate = pair * 2 + 1 - mine % 2

    def others(group):
        for a in group:
            send(a, mate)

        def more(n, carry):
            to = ((pair + 4 - n // 2) % 4) * 2 + n % 2
            for a in group:
                send(a, to)
            return carry

        lax.fori_loop(2, NWIN, more, 0)

    others((1, 2))
    others((0, 3))

    for c in locals_:
        c.wait()
    lane = lax.broadcasted_iota(jnp.int32, (1, LANES), 1)
    parity = ((lane // 32) % 2 * GROUP).astype(F32)
    first_half = lane < ROWS
    slot_base = lax.broadcasted_iota(jnp.int32, (32 * 24, 32), 1) * 128
    jrow = lax.broadcasted_iota(jnp.int32, (32, LANES), 0)
    jlane = lax.broadcasted_iota(jnp.int32, (32, LANES), 1)
    spots = jnp.zeros((32 * 24, LANES), F32) - parity
    for a in range(3):
        o = (idx_buf[:, a].reshape(32 * 24, 32) - slot_base).astype(F32).astype(BF16)
        at_a = jnp.where((jrow == jlane % 32) & ((jlane // 64) % 3 == a), 1.0, 0.0).astype(BF16)
        spots = spots + jnp.dot(o, at_a, preferred_element_type=F32)
    place[...] = spots.reshape(32, 24, LANES)
    sub = lax.broadcasted_iota(jnp.int32, (GROUP, LANES), 0).astype(F32)

    def halves(ref, r, row):
        return jnp.where(first_half, ref[r, pl.ds(row, 1), :], ref[r, pl.ds(row + 12, 1), :])

    def forward(t, carry):
        at = pl.multiple_of(t * 128, 128)
        pieces = []
        for bm in range(2):
            xt = drift_buf[:, pl.ds(at + bm * 768, 128)].astype(F32)
            pieces.append(jnp.dot(crow[...], xt, precision=HIGH, preferred_element_type=F32))
        y = jnp.concatenate(pieces, axis=0)
        u = lax.dot_general(ccol[...], y, (((1,), (1,)), ((), ())), precision=HIGH, preferred_element_type=F32)
        for bl in range(2):
            hit = jnp.where(sub == halves(place, rep, t * 2 + bl), u[bl * GROUP : (bl + 1) * GROUP, :], 0.0)
            picked[pl.ds(t * 2 + bl, 1), :] = jnp.sum(hit, axis=0, keepdims=True)
        return carry

    lax.fori_loop(0, 6, forward, 0)
    wl = lax.broadcasted_iota(jnp.int32, (LANES, 128), 0)
    nl = lax.broadcasted_iota(jnp.int32, (LANES, 128), 1)
    same = ((wl // 64) % 3 == nl // 32) & (wl % 32 == nl % 32)
    for bm in range(2):
        gather = jnp.where(same & (wl // ROWS == bm), 1.0, 0.0)
        kept[m, zlo, bm * 12 : bm * 12 + 12, :] = jnp.dot(
            picked[0:12, :], gather, precision=HIGH, preferred_element_type=F32
        )
    for k in range(1, 4):
        pltpu.make_async_remote_copy(
            src_ref=kept.at[m, zlo],
            dst_ref=kept.at[m, zlo],
            send_sem=ss_kept.at[0],
            recv_sem=rs_kept.at[0],
            device_id={"replica": rep_z(k)},
            device_id_type=MESH,
        ).start()

    scale = 1.0 / math.sqrt(HEAD)
    nt = (((1,), (1,)), ((), ()))

    def give(a, i):
        @pl.when(i == mine)
        def _():
            pltpu.make_async_copy(outb.at[a, rows_of(i), :], outs[a].at[0, :, cols_of(mine)], rs_out.at[a]).start()

        @pl.when(i != mine)
        def _():
            pltpu.make_async_remote_copy(
                src_ref=outb.at[a, rows_of(i), :],
                dst_ref=outs[a].at[0, :, cols_of(mine)],
                send_sem=ss_out.at[a],
                recv_sem=rs_out.at[a],
                device_id={"seq": base + i},
                device_id_type=MESH,
            ).start()

    for a in (1, 2):
        pltpu.make_async_copy(inb.at[a], inb.at[a], rs_kv.at[a - 1]).wait()
    for h in range(2):
        of_head = slice(h * HEAD, (h + 1) * HEAD)
        kt_buf[h] = jnp.transpose(inb[1, :, of_head].astype(F32)).astype(BF16)
    dk_acc[...] = jnp.zeros_like(dk_acc)
    dv_acc[...] = jnp.zeros_like(dv_acc)

    pltpu.make_async_copy(kept.at[m, 0:3], kept.at[m, 0:3], rs_kept.at[0]).wait()
    for k in range(1, 8):
        pltpu.make_async_remote_copy(
            src_ref=kept.at[m],
            dst_ref=kept.at[m],
            send_sem=ss_kept.at[1],
            recv_sem=rs_kept.at[1],
            device_id={"replica": rep_m(k)},
            device_id_type=MESH,
        ).start()

    def step(n, carry):
        b = (pair + n) % 4
        for u in range(2):
            i = b * 2 + u
            pltpu.make_async_copy(inb.at[0, rows_of(i)], inb.at[0, rows_of(i)], rs_q.at[i]).wait()
            pltpu.make_async_copy(inb.at[3, rows_of(i)], inb.at[3, rows_of(i)], rs_g.at[i]).wait()
        rows = pl.ds(pl.multiple_of(b * QB, QB), QB)
        for h in range(2):
            of_head = slice(h * HEAD, (h + 1) * HEAD)
            qb = inb[0, rows, of_head]
            gb = inb[3, rows, of_head]
            s = lax.dot_general(inb[1, :, of_head], qb, nt, preferred_element_type=F32)
            top = jnp.max(s, axis=0, keepdims=True)
            e = jnp.exp((s - top) * scale)
            p = e * (1.0 / jnp.sum(e, axis=0, keepdims=True))
            low = p.astype(BF16)
            d = lax.dot_general(inb[2, :, of_head], gb, nt, preferred_element_type=F32)
            delta = jnp.sum(low.astype(F32) * d, axis=0, keepdims=True)
            sg = (p * (d - delta)).astype(BF16)
            dqt = jnp.dot(kt_buf[h], sg, preferred_element_type=F32) * scale
            outb[0, rows, of_head] = jnp.transpose(dqt).astype(BF16)
            dv_acc[h] += jnp.dot(low, gb, preferred_element_type=F32)
            dk_acc[h] += jnp.dot(sg, qb, preferred_element_type=F32)
        for u in range(2):
            give(0, b * 2 + u)
        return carry

    lax.fori_loop(0, LEN // QB, step, 0)
    for h in range(2):
        of_head = slice(h * HEAD, (h + 1) * HEAD)
        outb[1, :, of_head] = (dk_acc[h] * scale).astype(BF16)
        outb[2, :, of_head] = dv_acc[h].astype(BF16)

    def rest(n, carry):
        i = ((pair + n // 2) % 4) * 2 + n % 2
        give(1, i)
        give(2, i)
        return carry

    lax.fori_loop(0, NWIN, rest, 0)

    pltpu.make_async_copy(kept.at[0:7], kept.at[0:7], rs_kept.at[1]).wait()
    nr = lax.broadcasted_iota(jnp.int32, (128, LANES), 0)
    wr = lax.broadcasted_iota(jnp.int32, (128, LANES), 1)
    widen = jnp.where(((wr // 64) % 3 == nr // 32) & (wr % 32 == nr % 32), 1.0, 0.0)

    def spread_out(i, carry):
        some = kept[i].reshape(4 * 24, 128)
        wide[pl.ds(i * 4, 4)] = jnp.dot(some, widen, precision=HIGH, preferred_element_type=F32).reshape(4, 24, LANES)
        return carry

    lax.fori_loop(0, 8, spread_out, 0)

    def backward(t, carry):
        at = pl.multiple_of(t * 128, 128)
        zs = []
        for bl in range(2):

            def add(i, z):
                for r in range(8):
                    slot = i * 8 + (r % 2) * 4 + r // 2
                    hit = sub == halves(place, i * 8 + r, t * 2 + bl)
                    z = z + jnp.where(hit, halves(wide, slot, t * 2 + bl), 0.0)
                return z

            zs.append(lax.fori_loop(0, 4, add, jnp.zeros((GROUP, LANES), F32)))
        z = jnp.transpose(jnp.concatenate(zs, axis=0))
        w = jnp.dot(z, ccol[...], precision=HIGH, preferred_element_type=F32)
        for bm in range(2):
            o = jnp.dot(crowt[...], w[bm * ROWS : (bm + 1) * ROWS, :], precision=HIGH, preferred_element_type=F32)
            outer_buf[:, pl.ds(at + bm * 768, 128)] = o.astype(BF16)
        return carry

    lax.fori_loop(0, 6, backward, 0)
    last = pltpu.make_async_copy(outer_buf, outer_ref, lsem.at[5])
    last.start()

    part = pl.ds(0, 7 * WIDE)
    for a in range(4):
        pltpu.make_async_copy(ins[a].at[0, :, part], ins[a].at[0, :, part], ss_in.at[a]).wait()
    pltpu.make_async_copy(kept.at[0, 0:3], kept.at[0, 0:3], ss_kept.at[0]).wait()
    pltpu.make_async_copy(kept.at[0:7], kept.at[0:7], ss_kept.at[1]).wait()
    for a in range(3):
        pltpu.make_async_copy(outs[a].at[0, :, part], outs[a].at[0, :, part], ss_out.at[a]).wait()
    for a in range(3):
        pltpu.make_async_copy(outs[a].at[0], outs[a].at[0], rs_out.at[a]).wait()
    last.wait()


def place_results(*refs):
    arrived, left = refs[12:]
    into = [pltpu.make_async_copy(refs[i], refs[8 + i], arrived.at[i]) for i in range(4)]
    out = [pltpu.make_async_copy(refs[8 + i], refs[4 + i], left.at[i]) for i in range(4)]
    for c in into:
        c.start()
    for i in range(4):
        into[i].wait()
        out[i].start()
    for c in out:
        c.wait()


def on_device(query_rows, key_rows, value_rows, out_grad, drift, kept_index):
    crow, crowt, ccol = (jnp.asarray(t) for t in tables())
    anyspec = pl.BlockSpec(memory_space=pl.ANY)
    rows = jax.ShapeDtypeStruct((1, TOK, 2048), BF16)
    results = (rows, rows, rows, jax.ShapeDtypeStruct((ROWS, COLS), BF16))
    landed = pl.pallas_call(
        kernel,
        out_shape=results,
        in_specs=[anyspec] * 9,
        out_specs=[anyspec] * 4,
        scratch_shapes=[
            pltpu.VMEM((4, LEN, WIDE), BF16),
            pltpu.VMEM((3, LEN, WIDE), BF16),
            pltpu.VMEM((2, HEAD, LEN), BF16),
            pltpu.VMEM((2, LEN, HEAD), F32),
            pltpu.VMEM((2, LEN, HEAD), F32),
            pltpu.VMEM((ROWS, COLS), BF16),
            pltpu.VMEM((32, 3, 24, 32), jnp.int32),
            pltpu.VMEM((ROWS, ROWS), F32),
            pltpu.VMEM((ROWS, ROWS), F32),
            pltpu.VMEM((128, 128), F32),
            pltpu.VMEM((8, 4, 24, 128), F32),
            pltpu.VMEM((16, LANES), F32),
            pltpu.VMEM((32, 24, LANES), F32),
            pltpu.VMEM((32, 24, LANES), F32),
            pltpu.VMEM((ROWS, COLS), BF16),
            pltpu.SemaphoreType.DMA((4,)),
            pltpu.SemaphoreType.DMA((2,)),
            pltpu.SemaphoreType.DMA((NWIN,)),
            pltpu.SemaphoreType.DMA((NWIN,)),
            pltpu.SemaphoreType.DMA((3,)),
            pltpu.SemaphoreType.DMA((3,)),
            pltpu.SemaphoreType.DMA((2,)),
            pltpu.SemaphoreType.DMA((2,)),
            pltpu.SemaphoreType.DMA((6,)),
        ],
        compiler_params=pltpu.CompilerParams(
            collective_id=0, has_side_effects=True, vmem_limit_bytes=63 << 20
        ),
    )(query_rows, key_rows, value_rows, out_grad, drift, kept_index, crow, crowt, ccol)
    return pl.pallas_call(
        place_results,
        out_shape=results,
        in_specs=[anyspec] * 4,
        out_specs=[anyspec] * 4,
        scratch_shapes=[pltpu.VMEM(r.shape, r.dtype) for r in results]
        + [pltpu.SemaphoreType.DMA((4,)), pltpu.SemaphoreType.DMA((4,))],
        compiler_params=pltpu.CompilerParams(vmem_limit_bytes=63 << 20),
    )(*landed)


def solution(mesh):
    tokens = P("replica", "seq", None)
    return jax.shard_map(
        on_device,
        mesh=mesh,
        in_specs=(tokens, tokens, tokens, tokens, tokens, P(None, "seq", None, None)),
        out_specs=(tokens, tokens, tokens, P("seq", None)),
        check_vma=False,
    )
```

```python
import functools
import math

import jax
import jax.numpy as jnp
import numpy as np
from jax import lax
from jax.experimental import pallas as pl
from jax.experimental.pallas import tpu as pltpu
from jax.sharding import PartitionSpec as P

MESH = pl.DeviceIdType.MESH
HEAD = 128
GROUP = 64
NWIN = 8
TOK = 128
LEN = NWIN * TOK
WIDE = 2 * HEAD
QB = 256
ROWS = 192
COLS = 1536
LANES = 384
F32 = jnp.float32
BF16 = jnp.bfloat16
HIGH = lax.Precision.HIGHEST


def tables():
    i = np.arange(GROUP)[:, None].astype(np.float64)
    j = np.arange(GROUP)[None, :].astype(np.float64)
    c = np.where(i == 0, math.sqrt(1.0 / GROUP), math.sqrt(2.0 / GROUP)) * np.cos(
        math.pi * (2.0 * j + 1.0) * i / (2.0 * GROUP)
    )
    perm = np.concatenate([c[0::2], c[1::2]], axis=0)
    crow = np.kron(np.eye(3), perm)
    ccol = np.kron(np.eye(2), c)
    return crow.astype(np.float32), crow.T.astype(np.float32).copy(), ccol.astype(np.float32)


def kernel(
    q_ref, k_ref, v_ref, g_ref, drift_ref, idx_ref, crow_ref, crowt_ref, ccol_ref,
    dq_ref, dk_ref, dv_ref, outer_ref,
    stage, inb, outb, kt_buf, dk_acc, dv_acc, drift_buf, idx_buf, crow, crowt, ccol, kept, picked, place, wide, outer_buf,
    ss_in, rs_kv, rs_q, ss_out, rs_out, ss_kept, rs_kept, lsem,
):
    rep = lax.axis_index("replica")
    seq = lax.axis_index("seq")
    base = (seq // NWIN) * NWIN
    mine = seq % NWIN
    pair = mine // 2
    x = rep // 8
    zlo = (rep // 2) % 4
    core = rep % 2
    m = x * 2 + core
    ins = (k_ref, v_ref, q_ref, g_ref)
    outs = (dq_ref, dk_ref, dv_ref)

    def rep_z(k):
        return x * 8 + ((zlo + k) % 4) * 2 + core

    def rep_m(k):
        m2 = (m + k) % 8
        return (m2 // 2) * 8 + zlo * 2 + m2 % 2

    def rows_of(i):
        return pl.ds(pl.multiple_of(i * TOK, TOK), TOK)

    def cols_of(i):
        return pl.ds(pl.multiple_of(i * WIDE, WIDE), WIDE)

    barrier = pltpu.get_barrier_semaphore()
    for k in range(1, NWIN):
        pl.semaphore_signal(barrier, inc=1, device_id={"seq": base + (mine + k) % NWIN}, device_id_type=MESH)
    for k in range(1, 4):
        pl.semaphore_signal(barrier, inc=1, device_id={"replica": rep_z(k)}, device_id_type=MESH)
    for k in range(1, 8):
        pl.semaphore_signal(barrier, inc=1, device_id={"replica": rep_m(k)}, device_id_type=MESH)

    locals_ = [
        pltpu.make_async_copy(drift_ref.at[0], drift_buf, lsem.at[0]),
        pltpu.make_async_copy(idx_ref, idx_buf, lsem.at[1]),
        pltpu.make_async_copy(crow_ref, crow, lsem.at[2]),
        pltpu.make_async_copy(crowt_ref, crowt, lsem.at[3]),
        pltpu.make_async_copy(ccol_ref, ccol, lsem.at[4]),
    ]
    for c in locals_:
        c.start()

    def stage_for(i, carry):
        for a in range(4):
            pltpu.make_async_copy(ins[a].at[0, :, cols_of(i)], stage.at[a, i], lsem.at[6]).start()
        return carry

    lax.fori_loop(0, NWIN, stage_for, 0)

    def arrival(group):
        return (rs_kv.at[0], rs_q.at[mine])[group]

    for a in range(4):
        pltpu.make_async_copy(ins[a].at[0, :, cols_of(mine)], inb.at[a, rows_of(mine), :], arrival(a // 2)).start()

    pltpu.make_async_copy(stage, stage, lsem.at[6]).wait()
    pl.semaphore_wait(barrier, 7 + 3 + 7)

    def send(group, to):
        pltpu.make_async_remote_copy(
            src_ref=stage.at[2 * group : 2 * group + 2, to],
            dst_ref=inb.at[2 * group : 2 * group + 2, rows_of(mine), :],
            send_sem=ss_in.at[group],
            recv_sem=arrival(group),
            device_id={"seq": base + to},
            device_id_type=MESH,
        ).start()

    mate = pair * 2 + 1 - mine % 2

    def others(group):
        send(group, mate)

        def more(n, carry):
            to = ((pair + 4 - n // 2) % 4) * 2 + n % 2
            send(group, to)
            return carry

        lax.fori_loop(2, NWIN, more, 0)

    others(0)
    others(1)

    for c in locals_:
        c.wait()
    lane = lax.broadcasted_iota(jnp.int32, (1, LANES), 1)
    parity = ((lane // 32) % 2 * GROUP).astype(F32)
    first_half = lane < ROWS
    slot_base = lax.broadcasted_iota(jnp.int32, (32 * 24, 32), 1) * 128
    jrow = lax.broadcasted_iota(jnp.int32, (32, LANES), 0)
    jlane = lax.broadcasted_iota(jnp.int32, (32, LANES), 1)
    spots = jnp.zeros((32 * 24, LANES), F32) - parity
    for a in range(3):
        o = (idx_buf[:, a].reshape(32 * 24, 32) - slot_base).astype(F32).astype(BF16)
        at_a = jnp.where((jrow == jlane % 32) & ((jlane // 64) % 3 == a), 1.0, 0.0).astype(BF16)
        spots = spots + jnp.dot(o, at_a, preferred_element_type=F32)
    place[...] = spots.reshape(32, 24, LANES)
    sub = lax.broadcasted_iota(jnp.int32, (GROUP, LANES), 0).astype(F32)

    def halves(ref, r, row):
        return jnp.where(first_half, ref[r, pl.ds(row, 1), :], ref[r, pl.ds(row + 12, 1), :])

    def forward(t, carry):
        at = pl.multiple_of(t * 128, 128)
        pieces = []
        for bm in range(2):
            xt = drift_buf[:, pl.ds(at + bm * 768, 128)].astype(F32)
            pieces.append(jnp.dot(crow[...], xt, precision=HIGH, preferred_element_type=F32))
        y = jnp.concatenate(pieces, axis=0)
        u = lax.dot_general(ccol[...], y, (((1,), (1,)), ((), ())), precision=HIGH, preferred_element_type=F32)
        for bl in range(2):
            hit = jnp.where(sub == halves(place, rep, t * 2 + bl), u[bl * GROUP : (bl + 1) * GROUP, :], 0.0)
            picked[pl.ds(t * 2 + bl, 1), :] = jnp.sum(hit, axis=0, keepdims=True)
        return carry

    lax.fori_loop(0, 6, forward, 0)
    wl = lax.broadcasted_iota(jnp.int32, (LANES, 128), 0)
    nl = lax.broadcasted_iota(jnp.int32, (LANES, 128), 1)
    same = ((wl // 64) % 3 == nl // 32) & (wl % 32 == nl % 32)
    for bm in range(2):
        gather = jnp.where(same & (wl // ROWS == bm), 1.0, 0.0)
        kept[m, zlo, bm * 12 : bm * 12 + 12, :] = jnp.dot(
            picked[0:12, :], gather, precision=HIGH, preferred_element_type=F32
        )
    for k in range(1, 4):
        pltpu.make_async_remote_copy(
            src_ref=kept.at[m, zlo],
            dst_ref=kept.at[m, zlo],
            send_sem=ss_kept.at[0],
            recv_sem=rs_kept.at[0],
            device_id={"replica": rep_z(k)},
            device_id_type=MESH,
        ).start()

    scale = 1.0 / math.sqrt(HEAD)
    nt = (((1,), (1,)), ((), ()))

    def give(a, i):
        @pl.when(i == mine)
        def _():
            pltpu.make_async_copy(outb.at[a, rows_of(i), :], outs[a].at[0, :, cols_of(mine)], rs_out.at[a]).start()

        @pl.when(i != mine)
        def _():
            pltpu.make_async_remote_copy(
                src_ref=outb.at[a, rows_of(i), :],
                dst_ref=outs[a].at[0, :, cols_of(mine)],
                send_sem=ss_out.at[a],
                recv_sem=rs_out.at[a],
                device_id={"seq": base + i},
                device_id_type=MESH,
            ).start()

    pltpu.make_async_copy(inb.at[0:2], inb.at[0:2], rs_kv.at[0]).wait()
    for h in range(2):
        of_head = slice(h * HEAD, (h + 1) * HEAD)
        kt_buf[h] = jnp.transpose(inb[0, :, of_head].astype(F32)).astype(BF16)
    dk_acc[...] = jnp.zeros_like(dk_acc)
    dv_acc[...] = jnp.zeros_like(dv_acc)

    pltpu.make_async_copy(kept.at[m, 0:3], kept.at[m, 0:3], rs_kept.at[0]).wait()
    for k in range(1, 8):
        pltpu.make_async_remote_copy(
            src_ref=kept.at[m],
            dst_ref=kept.at[m],
            send_sem=ss_kept.at[1],
            recv_sem=rs_kept.at[1],
            device_id={"replica": rep_m(k)},
            device_id_type=MESH,
        ).start()

    def step(n, carry):
        b = (pair + n) % 4
        for u in range(2):
            i = b * 2 + u
            pltpu.make_async_copy(inb.at[2:4, rows_of(i)], inb.at[2:4, rows_of(i)], rs_q.at[i]).wait()
        rows = pl.ds(pl.multiple_of(b * QB, QB), QB)
        for h in range(2):
            of_head = slice(h * HEAD, (h + 1) * HEAD)
            qb = inb[2, rows, of_head]
            gb = inb[3, rows, of_head]
            s = lax.dot_general(inb[0, :, of_head], qb, nt, preferred_element_type=F32)
            top = jnp.max(s, axis=0, keepdims=True)
            e = jnp.exp((s - top) * scale)
            p = e * (1.0 / jnp.sum(e, axis=0, keepdims=True))
            low = p.astype(BF16)
            d = lax.dot_general(inb[1, :, of_head], gb, nt, preferred_element_type=F32)
            delta = jnp.sum(low.astype(F32) * d, axis=0, keepdims=True)
            sg = (p * (d - delta)).astype(BF16)
            dqt = jnp.dot(kt_buf[h], sg, preferred_element_type=F32) * scale
            outb[0, rows, of_head] = jnp.transpose(dqt).astype(BF16)
            dv_acc[h] += jnp.dot(low, gb, preferred_element_type=F32)
            dk_acc[h] += jnp.dot(sg, qb, preferred_element_type=F32)
        for u in range(2):
            give(0, b * 2 + u)
        return carry

    lax.fori_loop(0, LEN // QB, step, 0)
    for h in range(2):
        of_head = slice(h * HEAD, (h + 1) * HEAD)
        outb[1, :, of_head] = (dk_acc[h] * scale).astype(BF16)
        outb[2, :, of_head] = dv_acc[h].astype(BF16)

    def rest(n, carry):
        i = ((pair + n // 2) % 4) * 2 + n % 2
        give(1, i)
        give(2, i)
        return carry

    lax.fori_loop(0, NWIN, rest, 0)

    pltpu.make_async_copy(kept.at[0:7], kept.at[0:7], rs_kept.at[1]).wait()
    nr = lax.broadcasted_iota(jnp.int32, (128, LANES), 0)
    wr = lax.broadcasted_iota(jnp.int32, (128, LANES), 1)
    widen = jnp.where(((wr // 64) % 3 == nr // 32) & (wr % 32 == nr % 32), 1.0, 0.0)

    def spread_out(i, carry):
        some = kept[i].reshape(4 * 24, 128)
        wide[pl.ds(i * 4, 4)] = jnp.dot(some, widen, precision=HIGH, preferred_element_type=F32).reshape(4, 24, LANES)
        return carry

    lax.fori_loop(0, 8, spread_out, 0)

    def backward(t, carry):
        at = pl.multiple_of(t * 128, 128)
        zs = []
        for bl in range(2):

            def add(i, z):
                for r in range(8):
                    slot = i * 8 + (r % 2) * 4 + r // 2
                    hit = sub == halves(place, i * 8 + r, t * 2 + bl)
                    z = z + jnp.where(hit, halves(wide, slot, t * 2 + bl), 0.0)
                return z

            zs.append(lax.fori_loop(0, 4, add, jnp.zeros((GROUP, LANES), F32)))
        z = jnp.transpose(jnp.concatenate(zs, axis=0))
        w = jnp.dot(z, ccol[...], precision=HIGH, preferred_element_type=F32)
        for bm in range(2):
            o = jnp.dot(crowt[...], w[bm * ROWS : (bm + 1) * ROWS, :], precision=HIGH, preferred_element_type=F32)
            outer_buf[:, pl.ds(at + bm * 768, 128)] = o.astype(BF16)
        return carry

    lax.fori_loop(0, 6, backward, 0)
    last = pltpu.make_async_copy(outer_buf, outer_ref, lsem.at[5])
    last.start()

    part = pl.ds(0, 7 * WIDE)
    for group in range(2):
        pltpu.make_async_copy(stage.at[0:2, 0:7], stage.at[0:2, 0:7], ss_in.at[group]).wait()
    pltpu.make_async_copy(kept.at[0, 0:3], kept.at[0, 0:3], ss_kept.at[0]).wait()
    pltpu.make_async_copy(kept.at[0:7], kept.at[0:7], ss_kept.at[1]).wait()
    for a in range(3):
        pltpu.make_async_copy(outs[a].at[0, :, part], outs[a].at[0, :, part], ss_out.at[a]).wait()
    for a in range(3):
        pltpu.make_async_copy(outs[a].at[0], outs[a].at[0], rs_out.at[a]).wait()
    last.wait()


def place_results(*refs):
    arrived, left = refs[12:]
    into = [pltpu.make_async_copy(refs[i], refs[8 + i], arrived.at[i]) for i in range(4)]
    out = [pltpu.make_async_copy(refs[8 + i], refs[4 + i], left.at[i]) for i in range(4)]
    for c in into:
        c.start()
    for i in range(4):
        into[i].wait()
        out[i].start()
    for c in out:
        c.wait()


def on_device(query_rows, key_rows, value_rows, out_grad, drift, kept_index):
    crow, crowt, ccol = (jnp.asarray(t) for t in tables())
    anyspec = pl.BlockSpec(memory_space=pl.ANY)
    rows = jax.ShapeDtypeStruct((1, TOK, 2048), BF16)
    results = (rows, rows, rows, jax.ShapeDtypeStruct((ROWS, COLS), BF16))
    landed = pl.pallas_call(
        kernel,
        out_shape=results,
        in_specs=[anyspec] * 9,
        out_specs=[anyspec] * 4,
        scratch_shapes=[
            pltpu.VMEM((4, NWIN, TOK, WIDE), BF16),
            pltpu.VMEM((4, LEN, WIDE), BF16),
            pltpu.VMEM((3, LEN, WIDE), BF16),
            pltpu.VMEM((2, HEAD, LEN), BF16),
            pltpu.VMEM((2, LEN, HEAD), F32),
            pltpu.VMEM((2, LEN, HEAD), F32),
            pltpu.VMEM((ROWS, COLS), BF16),
            pltpu.VMEM((32, 3, 24, 32), jnp.int32),
            pltpu.VMEM((ROWS, ROWS), F32),
            pltpu.VMEM((ROWS, ROWS), F32),
            pltpu.VMEM((128, 128), F32),
            pltpu.VMEM((8, 4, 24, 128), F32),
            pltpu.VMEM((16, LANES), F32),
            pltpu.VMEM((32, 24, LANES), F32),
            pltpu.VMEM((32, 24, LANES), F32),
            pltpu.VMEM((ROWS, COLS), BF16),
            pltpu.SemaphoreType.DMA((2,)),
            pltpu.SemaphoreType.DMA((1,)),
            pltpu.SemaphoreType.DMA((NWIN,)),
            pltpu.SemaphoreType.DMA((3,)),
            pltpu.SemaphoreType.DMA((3,)),
            pltpu.SemaphoreType.DMA((2,)),
            pltpu.SemaphoreType.DMA((2,)),
            pltpu.SemaphoreType.DMA((7,)),
        ],
        compiler_params=pltpu.CompilerParams(
            collective_id=0, has_side_effects=True, vmem_limit_bytes=63 << 20
        ),
    )(query_rows, key_rows, value_rows, out_grad, drift, kept_index, crow, crowt, ccol)
    return pl.pallas_call(
        place_results,
        out_shape=results,
        in_specs=[anyspec] * 4,
        out_specs=[anyspec] * 4,
        scratch_shapes=[pltpu.VMEM(r.shape, r.dtype) for r in results]
        + [pltpu.SemaphoreType.DMA((4,)), pltpu.SemaphoreType.DMA((4,))],
        compiler_params=pltpu.CompilerParams(vmem_limit_bytes=63 << 20),
    )(*landed)


def solution(mesh):
    tokens = P("replica", "seq", None)
    return jax.shard_map(
        on_device,
        mesh=mesh,
        in_specs=(tokens, tokens, tokens, tokens, tokens, P(None, "seq", None, None)),
        out_specs=(tokens, tokens, tokens, P("seq", None)),
        check_vma=False,
    )
```
